32 devices in a mesh: blk: 16 (over z, x, core), col: 2 (over y).
Axes of the slice: x: 2, y: 2, z: 4, core: 2. Of those that a mesh axis runs over, the one named last changes fastest.
Arguments:
- targets: bfloat16 [16, 48, 72, 96], P('blk'), may hold values from -6 to 6
- sources: bfloat16 [64, 48, 72, 96], P(('blk', 'col')), may hold values from -6 to 6
- band_of_slot: int32 [64], P(('blk', 'col')), may hold values from 0 to 63, each once
- occupied: int32 [64], replicated, may hold values 0 or 1
Outputs:
- fock: float32 [16, 48, 72, 96], P('blk', 'col')
The draws below stay inside these ranges and needn't reach their ends.
Inputs may be any that keep to these rules, and one draw needn't show every extreme that they name: `band_of_slot`: every band number appears in exactly one slot.
All inputs are finite; a program needn't handle non-finite values.
Results may differ from the reference program's by a relative error of at most 0.0003.
Values may be sent and summed in bfloat16 or wider, within the bound.
A program may use at most 64 MiB of HBM per device.

```python
import math
import jax
import jax.numpy as jnp
from jax import lax

NX = 48
NY = 72
NZ = 96
TARG_DEV = 1
SRC_DEV = 2
HOPS = 2
BANDS = 16
SOURCES = 64
N_BLK = 16
N_COL = 2


def plant(values, key, smallest, high):
    place = [jax.random.randint(jax.random.fold_in(key, axis), (), 0, length) for axis, length in enumerate(values.shape)]
    longest = values.shape.index(max(values.shape))
    next_to = place[:longest] + [(place[longest] + 1) % values.shape[longest]] + place[longest + 1:]
    return values.at[tuple(place)].set(smallest).at[tuple(next_to)].set(high)


def steps_of(rng, dims, cuts, low, high):
    def one(axis_at, shards_of):
        steps = jax.random.uniform(jax.random.fold_in(jax.random.fold_in(rng, 6), axis_at), (shards_of,), jnp.float32, low / len(cuts), high / len(cuts))
        return jnp.repeat(jnp.exp(steps), dims[axis_at] // shards_of).reshape((-1,) + (1,) * (len(dims) - axis_at - 1))

    factor_of = one(*cuts[0])
    for cut in cuts[1:]:
        factor_of = factor_of * one(*cut)
    return factor_of


def centred(own_key, shape, deviation, most, cuts=(), held_as=jnp.bfloat16):
    values = deviation * jax.random.normal(own_key, shape, jnp.float32)
    if cuts:
        values = values * steps_of(own_key, shape, cuts, -0.22, 0.18)
    return jnp.clip(values, -most, most).astype(held_as)


def setup_inputs(seed: int = 0) -> dict:
    key_list = jax.random.split(jax.random.key(seed), 5)
    return {
        "targets": centred(key_list[0], (BANDS, NX, NY, NZ), 1.0, 6.0, ((0, 16),)),
        "sources": centred(key_list[1], (SOURCES, NX, NY, NZ), 1.0, 6.0, ((0, 32),)),
        "band_of_slot": jax.random.permutation(key_list[2], SOURCES).astype(jnp.int32),
        "occupied": plant((jax.random.randint(key_list[3], (SOURCES,), 0, 4) < 3).astype(jnp.int32), jax.random.fold_in(key_list[3], 1), 0, 1),
    }


grid_spacing = 0.3
screening = 0.11


def frequency_sq(length):
    index_row = jnp.arange(length, dtype=jnp.int32)
    periodic = jnp.minimum(index_row, length - index_row).astype(jnp.float32)
    return (2.0 * math.pi * periodic / (length * grid_spacing)) ** 2


def kernel_field(size_x, size_y, size_z):
    g_sq = frequency_sq(size_x)[:, None, None] + frequency_sq(size_y)[None, :, None] + frequency_sq(size_z)[None, None, :]
    safe_sq = jnp.where(g_sq > 0, g_sq, jnp.float32(1.0))
    value = 4.0 * math.pi / safe_sq * (1.0 - jnp.exp(-safe_sq / (4.0 * screening * screening)))
    return jnp.where(g_sq > 0, value, jnp.float32(math.pi / (screening * screening))).astype(jnp.float32)


def reference(targets, sources, band_of_slot, occupied):
    weights = jnp.where(occupied[band_of_slot] > 0, 1.0, 0.0).astype(jnp.float32)
    per_block = N_COL * SRC_DEV
    src_blocks = sources.astype(jnp.float32).reshape(N_BLK, per_block, NX, NY, NZ)
    weight_blocks = weights.reshape(N_BLK, per_block)
    coulomb = kernel_field(NX, NY, NZ)[:, :, : NZ // 2 + 1]

    def one_target(band_index):
        psi = targets[band_index].astype(jnp.float32)
        block_index = band_index // TARG_DEV
        accum = jnp.zeros((NX, NY, NZ), jnp.float32)
        for hop_index in range(HOPS + 1):
            src_index = (block_index - hop_index) % N_BLK
            orbitals = src_blocks[src_index]
            occup = weight_blocks[src_index]
            pair_field = psi[None] * orbitals
            spectrum = jnp.fft.rfftn(pair_field, axes=(1, 2, 3))
            potential = jnp.fft.irfftn(spectrum * coulomb, s=(NX, NY, NZ), axes=(1, 2, 3))
            accum = accum + jnp.sum(potential * orbitals * occup[:, None, None, None], axis=0)
        return -0.125 * accum

    return lax.map(one_target, jnp.arange(BANDS, dtype=jnp.int32))
```

```python
import functools
import math

import jax
import jax.numpy as jnp
import ml_dtypes
import numpy as np
from jax import lax
from jax.experimental import pallas as pl
from jax.experimental.pallas import tpu as pltpu
from jax.sharding import PartitionSpec as P

HOPS = 2
LANES = 128

grid_spacing = 0.3
screening = 0.11


def passed_along(value, axis, steps):
    count = lax.axis_size(axis)
    pairs = [(source, (source + steps) % count) for source in range(count)]
    return lax.ppermute(value, axis, pairs)


def frequency_sq(length):
    index_row = np.arange(length)
    periodic = np.minimum(index_row, length - index_row).astype(np.float64)
    return (2.0 * math.pi * periodic / (length * grid_spacing)) ** 2


def kernel_table(size_x, size_y, size_z):
    g_sq = (
        frequency_sq(size_x)[:, None, None]
        + frequency_sq(size_y)[None, :, None]
        + frequency_sq(size_z)[None, None, :]
    )
    safe_sq = np.where(g_sq > 0, g_sq, 1.0)
    value = 4.0 * math.pi / safe_sq * (1.0 - np.exp(-safe_sq / (4.0 * screening * screening)))
    value = np.where(g_sq > 0, value, math.pi / (screening * screening))
    padded = np.zeros((size_x, size_y, LANES), np.float32)
    padded[:, :, :size_z] = value
    return padded.reshape(size_x, size_y * LANES)


def fourier_basis(length):
    row_index = np.arange(length)[:, None]
    col_index = np.arange(length)[None, :]
    residue = row_index * col_index % length
    phase_angle = 2.0 * math.pi / length * residue
    half_length = length // 2
    basis_table = np.where(row_index <= half_length, np.cos(phase_angle), np.sin(phase_angle))
    edge_row = (row_index == 0) | (row_index == half_length)
    norm_scale = np.where(edge_row, math.sqrt(1.0 / length), math.sqrt(2.0 / length))
    return basis_table * norm_scale


def two_parts(table):
    high = table.astype(ml_dtypes.bfloat16)
    low = (table - high.astype(np.float64)).astype(ml_dtypes.bfloat16)
    return high, low


def left_table(table):
    high, low = two_parts(table)
    return np.concatenate([high, high, low], axis=1)


def right_table(table):
    high, low = two_parts(table)
    length = table.shape[0]
    out = np.zeros((2 * LANES, 2 * LANES), ml_dtypes.bfloat16)
    for start in (0, LANES):
        out[start:start + length, :length] = high
        out[start:start + length, LANES:LANES + length] = low
    return out


def split(value):
    high = value.astype(jnp.bfloat16).astype(jnp.float32)
    return high, value - high


def dot(left, right):
    return jnp.dot(left, right, preferred_element_type=jnp.float32)


def along_rows(table, value):
    high, low = split(value)
    stacked = jnp.concatenate([high, low, high], axis=0).astype(jnp.bfloat16)
    return dot(table, stacked)


def along_lanes(value, table):
    high, low = split(value)
    wide = jnp.concatenate([high, low], axis=1).astype(jnp.bfloat16)
    product = dot(wide, table)
    return product[:, :LANES] + product[:, LANES:]


def exchange_kernel(
    has_accum, group_x, group_y, weight_ref, target_ref, source_ref, *refs
):
    if has_accum:
        accum_ref, *refs = refs
    coulomb_ref, x_in, x_out, y_in, y_out, z_in, z_out, out_ref, scratch = refs
    count_s, size_x, size_y, size_z = source_ref.shape
    rows = group_x * size_y

    def slabs(ref, start):
        return ref[pl.ds(start, group_x)].astype(jnp.float32).reshape(rows, size_z)

    @pl.loop(0, size_x // group_x)
    def _(step):
        start = step * group_x
        target = slabs(target_ref, start)
        for s in range(count_s):
            pair = target * slabs(source_ref.at[s], start)
            pair = jnp.concatenate(
                [pair, jnp.zeros((rows, LANES - size_z), jnp.float32)], axis=1
            )
            pair = along_lanes(pair, z_in[...])
            wide = jnp.concatenate(
                [pair[g * size_y:(g + 1) * size_y] for g in range(group_x)], axis=1
            )
            wide = along_rows(y_in[...], wide)
            for g in range(group_x):
                first = pl.multiple_of((start + g) * size_y, 8)
                scratch[s, pl.ds(first, size_y), :] = wide[:, g * LANES:(g + 1) * LANES]

    @pl.loop(0, size_y // group_y)
    def _(step):
        start = step * group_y
        columns = pl.ds(pl.multiple_of(start * LANES, LANES), group_y * LANES)
        for s in range(count_s):
            wide = jnp.concatenate(
                [
                    scratch[s, pl.ds(start + g, size_x, stride=size_y), :]
                    for g in range(group_y)
                ],
                axis=1,
            )
            wide = along_rows(x_in[...], wide) * coulomb_ref[:, columns]
            wide = along_rows(x_out[...], wide)
            for g in range(group_y):
                scratch[s, pl.ds(start + g, size_x, stride=size_y), :] = wide[
                    :, g * LANES:(g + 1) * LANES
                ]

    @pl.loop(0, size_x // group_x)
    def _(step):
        start = step * group_x
        total = None
        for s in range(count_s):
            wide = jnp.concatenate(
                [
                    scratch[s, pl.ds(pl.multiple_of((start + g) * size_y, 8), size_y), :]
                    for g in range(group_x)
                ],
                axis=1,
            )
            wide = along_rows(y_out[...], wide)
            field = jnp.concatenate(
                [wide[:, g * LANES:(g + 1) * LANES] for g in range(group_x)], axis=0
            )
            field = along_lanes(field, z_out[...])[:, :size_z]
            term = field * (slabs(source_ref.at[s], start) * weight_ref[s])
            total = term if total is None else total + term
        total = total.reshape(group_x, size_y, size_z)
        if has_accum:
            total = total + accum_ref[pl.ds(start, group_x)]
        out_ref[pl.ds(start, group_x)] = total


def largest_divisor(length, most):
    return max(d for d in range(1, most + 1) if length % d == 0)


def exchange(target, sources, weights, accum, tables):
    count_s, size_x, size_y, size_z = sources.shape
    vmem = pl.BlockSpec(memory_space=pltpu.VMEM)
    smem = pl.BlockSpec(memory_space=pltpu.SMEM)
    operands = [weights, target, sources]
    if accum is not None:
        operands.append(accum)
    operands += tables
    cells = size_x * size_y * size_z
    return pl.pallas_call(
        functools.partial(
            exchange_kernel,
            accum is not None,
            largest_divisor(size_x, 4),
            largest_divisor(size_y, 8),
        ),
        out_shape=jax.ShapeDtypeStruct((size_x, size_y, size_z), jnp.float32),
        in_specs=[smem] + [vmem] * (len(operands) - 1),
        out_specs=vmem,
        scratch_shapes=[pltpu.VMEM((count_s, size_x * size_y, LANES), jnp.float32)],
        compiler_params=pltpu.CompilerParams(vmem_limit_bytes=48 * 1024 * 1024),
        cost_estimate=pl.CostEstimate(
            flops=count_s * cells * 12 * (size_x + size_y + size_z),
            bytes_accessed=cells * (4 * count_s + 10),
            transcendentals=0,
        ),
    )(*operands)


def shards(targets, sources, band_of_slot, occupied):
    size_x, size_y, size_z = targets.shape[1:]
    basis_x, basis_y, basis_z = (fourier_basis(n) for n in (size_x, size_y, size_z))
    tables = [
        jnp.asarray(table)
        for table in (
            kernel_table(size_x, size_y, size_z),
            left_table(basis_x),
            left_table(basis_x.T),
            left_table(basis_y),
            left_table(basis_y.T),
            right_table(basis_z.T),
            right_table(basis_z),
        )
    ]
    band_ids = jnp.arange(occupied.shape[0], dtype=jnp.int32)
    matches = band_of_slot[:, None] == band_ids[None, :]
    weights = jnp.sum(jnp.where(matches, occupied[None, :], 0), axis=1).astype(jnp.bfloat16)
    moving = [(sources, weights)]
    for _ in range(HOPS):
        moving.append(passed_along(moving[-1], "blk", 1))
    fields = []
    for t in range(targets.shape[0]):
        accum = None
        for src, wts in moving:
            scaled = -0.125 * wts.astype(jnp.float32)
            accum = exchange(targets[t], src, scaled, accum, tables)
        fields.append(accum)
    return lax.psum_scatter(jnp.stack(fields), "col", scatter_dimension=1, tiled=True)


def solution(mesh):
    return jax.shard_map(
        shards,
        mesh=mesh,
        in_specs=(
            P("blk", None, None, None),
            P(("blk", "col"), None, None, None),
            P(("blk", "col")),
            P(),
        ),
        out_specs=P("blk", "col", None, None),
        check_vma=False,
    )
```

```python
import functools
import math

import jax
import jax.numpy as jnp
import ml_dtypes
import numpy as np
from jax import lax
from jax.experimental import pallas as pl
from jax.experimental.pallas import tpu as pltpu
from jax.sharding import PartitionSpec as P

HOPS = 2
LANES = 128

grid_spacing = 0.3
screening = 0.11


def frequency_sq(length):
    index_row = np.arange(length)
    periodic = np.minimum(index_row, length - index_row).astype(np.float64)
    return (2.0 * math.pi * periodic / (length * grid_spacing)) ** 2


def kernel_table(size_x, size_y, size_z):
    g_sq = (
        frequency_sq(size_x)[:, None, None]
        + frequency_sq(size_y)[None, :, None]
        + frequency_sq(size_z)[None, None, :]
    )
    safe_sq = np.where(g_sq > 0, g_sq, 1.0)
    value = 4.0 * math.pi / safe_sq * (1.0 - np.exp(-safe_sq / (4.0 * screening * screening)))
    value = np.where(g_sq > 0, value, math.pi / (screening * screening))
    padded = np.zeros((size_x, size_y, LANES), np.float32)
    padded[:, :, :size_z] = value
    return padded.reshape(size_x, size_y * LANES)


def fourier_basis(length):
    row_index = np.arange(length)[:, None]
    col_index = np.arange(length)[None, :]
    residue = row_index * col_index % length
    phase_angle = 2.0 * math.pi / length * residue
    half_length = length // 2
    basis_table = np.where(row_index <= half_length, np.cos(phase_angle), np.sin(phase_angle))
    edge_row = (row_index == 0) | (row_index == half_length)
    norm_scale = np.where(edge_row, math.sqrt(1.0 / length), math.sqrt(2.0 / length))
    return basis_table * norm_scale


def two_parts(table):
    high = table.astype(ml_dtypes.bfloat16)
    low = (table - high.astype(np.float64)).astype(ml_dtypes.bfloat16)
    return high, low


def left_table(table):
    high, low = two_parts(table)
    return np.concatenate([high, high, low], axis=1)


def right_table(table):
    high, low = two_parts(table)
    length = table.shape[0]
    out = np.zeros((2 * LANES, 2 * LANES), ml_dtypes.bfloat16)
    for start in (0, LANES):
        out[start:start + length, :length] = high
        out[start:start + length, LANES:LANES + length] = low
    return out


def split(value):
    high = value.astype(jnp.bfloat16).astype(jnp.float32)
    return high, value - high


def dot(left, right):
    return jnp.dot(left, right, preferred_element_type=jnp.float32)


def along_rows(table, value):
    high, low = split(value)
    stacked = jnp.concatenate([high, low, high], axis=0).astype(jnp.bfloat16)
    return dot(table, stacked)


def along_lanes(value, table):
    high, low = split(value)
    wide = jnp.concatenate([high, low], axis=1).astype(jnp.bfloat16)
    product = dot(wide, table)
    return product[:, :LANES] + product[:, LANES:]


def largest_divisor(length, most):
    return max(d for d in range(1, most + 1) if length % d == 0)


def exchange_kernel(
    count_blk,
    count_col,
    weight_hbm,
    target_hbm,
    source_hbm,
    *refs,
):
    tables_hbm, (out_ref,), refs = refs[:7], refs[7:8], refs[8:]
    (coulomb_ref, x_in, x_out, y_in, y_out, z_in, z_out), refs = refs[:7], refs[7:]
    (
        target_ref, held, weights, scratch, accum, landed,
        local_sem, hop_send, hop_recv, weight_send, weight_recv, part_send, part_recv,
    ) = refs
    _, count_s, size_x, size_y, size_z = held.shape
    part_x = size_x // count_col
    group_x = largest_divisor(part_x, 4)
    group_y = largest_divisor(size_y, 8)
    rows = group_x * size_y
    me_blk, me_col = lax.axis_index("blk"), lax.axis_index("col")
    right = lax.rem(me_blk + 1, count_blk)
    left = lax.rem(me_blk + count_blk - 1, count_blk)

    local = [
        pltpu.make_async_copy(source, dest, local_sem.at[index])
        for index, (source, dest) in enumerate(
            [(source_hbm, held.at[0]), (weight_hbm, weights.at[0]), (target_hbm, target_ref)]
            + list(
                zip(tables_hbm, (coulomb_ref, x_in, x_out, y_in, y_out, z_in, z_out))
            )
        )
    ]
    for copy in local:
        copy.start()

    barrier = pltpu.get_barrier_semaphore()
    others = [(right, me_col), (left, me_col)] + [
        (me_blk, lax.rem(me_col + d, count_col)) for d in range(1, count_col)
    ]
    for other in others:
        pl.semaphore_signal(
            barrier, inc=1, device_id=other, device_id_type=pl.DeviceIdType.MESH
        )
    pl.semaphore_wait(barrier, len(others))

    def hop_copies(hop):
        return [
            pltpu.make_async_remote_copy(
                src_ref=ref.at[hop],
                dst_ref=ref.at[hop + 1],
                send_sem=send.at[hop],
                recv_sem=recv.at[hop],
                device_id=(right, me_col),
                device_id_type=pl.DeviceIdType.MESH,
            )
            for ref, send, recv in (
                (held, hop_send, hop_recv), (weights, weight_send, weight_recv)
            )
        ]

    def part_copy(d):
        other = lax.rem(me_col + d, count_col)
        return pltpu.make_async_remote_copy(
            src_ref=accum.at[pl.ds(other * part_x, part_x)],
            dst_ref=landed.at[d - 1],
            send_sem=part_send.at[d - 1],
            recv_sem=part_recv.at[d - 1],
            device_id=(me_blk, other),
            device_id_type=pl.DeviceIdType.MESH,
        )

    local[0].wait()
    local[1].wait()
    for copy in hop_copies(0):
        copy.start()
    for copy in local[2:]:
        copy.wait()

    def slabs(ref, start):
        return ref[pl.ds(start, group_x)].astype(jnp.float32).reshape(rows, size_z)

    def to_spectrum(hop):
        @pl.loop(0, size_x // group_x)
        def _(step):
            start = step * group_x
            target = slabs(target_ref, start)
            for s in range(count_s):
                pair = target * slabs(held.at[hop, s], start)
                pair = jnp.concatenate(
                    [pair, jnp.zeros((rows, LANES - size_z), jnp.float32)], axis=1
                )
                pair = along_lanes(pair, z_in[...])
                wide = jnp.concatenate(
                    [pair[g * size_y:(g + 1) * size_y] for g in range(group_x)], axis=1
                )
                wide = along_rows(y_in[...], wide)
                for g in range(group_x):
                    first = pl.multiple_of((start + g) * size_y, 8)
                    scratch[s, pl.ds(first, size_y), :] = wide[:, g * LANES:(g + 1) * LANES]

        @pl.loop(0, size_y // group_y)
        def _(step):
            start = step * group_y
            columns = pl.ds(pl.multiple_of(start * LANES, LANES), group_y * LANES)
            for s in range(count_s):
                wide = jnp.concatenate(
                    [
                        scratch[s, pl.ds(start + g, size_x, stride=size_y), :]
                        for g in range(group_y)
                    ],
                    axis=1,
                )
                wide = along_rows(x_in[...], wide) * coulomb_ref[:, columns]
                wide = along_rows(x_out[...], wide)
                for g in range(group_y):
                    scratch[s, pl.ds(start + g, size_x, stride=size_y), :] = wide[
                        :, g * LANES:(g + 1) * LANES
                    ]

    def to_grid(hop, first_x, steps, fresh):
        @pl.loop(0, steps)
        def _(step):
            start = first_x + step * group_x
            total = None
            for s in range(count_s):
                wide = jnp.concatenate(
                    [
                        scratch[s, pl.ds(pl.multiple_of((start + g) * size_y, 8), size_y), :]
                        for g in range(group_x)
                    ],
                    axis=1,
                )
                wide = along_rows(y_out[...], wide)
                field = jnp.concatenate(
                    [wide[:, g * LANES:(g + 1) * LANES] for g in range(group_x)], axis=0
                )
                field = along_lanes(field, z_out[...])[:, :size_z]
                weight = weights[hop, s:s + 1, :size_z]
                term = field * (slabs(held.at[hop, s], start) * weight)
                total = term if total is None else total + term
            total = total.reshape(group_x, size_y, size_z)
            if not fresh:
                total = total + accum[pl.ds(start, group_x)]
            accum[pl.ds(start, group_x)] = total

    for hop in range(HOPS):
        to_spectrum(hop)
        to_grid(hop, 0, size_x // group_x, hop == 0)
        for copy in hop_copies(hop):
            copy.wait()
        if hop + 1 < HOPS:
            for copy in hop_copies(hop + 1):
                copy.start()

    to_spectrum(HOPS)
    for d in range(1, count_col):
        other = lax.rem(me_col + d, count_col)
        to_grid(HOPS, other * part_x, part_x // group_x, False)
        part_copy(d).start()
    to_grid(HOPS, me_col * part_x, part_x // group_x, False)
    for d in range(1, count_col):
        part_copy(d).wait()

    @pl.loop(0, part_x)
    def _(step):
        total = accum[me_col * part_x + step]
        for d in range(1, count_col):
            total = total + landed[d - 1, step]
        out_ref[step] = total


def exchange(target, sources, weights, tables):
    count_s, size_x, size_y, size_z = sources.shape
    count_blk, count_col = lax.axis_size("blk"), lax.axis_size("col")
    part_x = size_x // count_col
    operands = [weights, target, sources] + tables
    cells = size_x * size_y * size_z
    dma = pltpu.SemaphoreType.DMA
    return pl.pallas_call(
        functools.partial(exchange_kernel, count_blk, count_col),
        out_shape=jax.ShapeDtypeStruct((part_x, size_y, size_z), jnp.float32),
        in_specs=[pl.BlockSpec(memory_space=pl.ANY)] * len(operands),
        out_specs=pl.BlockSpec(memory_space=pltpu.VMEM),
        scratch_shapes=[pltpu.VMEM(table.shape, table.dtype) for table in tables]
        + [
            pltpu.VMEM(target.shape, target.dtype),
            pltpu.VMEM((HOPS + 1,) + sources.shape, sources.dtype),
            pltpu.VMEM((HOPS + 1,) + weights.shape, weights.dtype),
            pltpu.VMEM((count_s, size_x * size_y, LANES), jnp.float32),
            pltpu.VMEM((size_x, size_y, size_z), jnp.float32),
            pltpu.VMEM((max(count_col - 1, 1), part_x, size_y, size_z), jnp.float32),
            dma((len(operands),)),
            dma((HOPS,)),
            dma((HOPS,)),
            dma((HOPS,)),
            dma((HOPS,)),
            dma((max(count_col - 1, 1),)),
            dma((max(count_col - 1, 1),)),
        ],
        compiler_params=pltpu.CompilerParams(
            vmem_limit_bytes=56 * 1024 * 1024, collective_id=0, has_side_effects=True
        ),
        cost_estimate=pl.CostEstimate(
            flops=(HOPS + 1) * count_s * cells * 12 * (size_x + size_y + size_z),
            bytes_accessed=cells * (4 * count_s + 10),
            transcendentals=0,
        ),
    )(*operands)


def shards(targets, sources, band_of_slot, occupied):
    size_x, size_y, size_z = targets.shape[1:]
    basis_x, basis_y, basis_z = (fourier_basis(n) for n in (size_x, size_y, size_z))
    tables = [
        jnp.asarray(table)
        for table in (
            kernel_table(size_x, size_y, size_z),
            left_table(basis_x),
            left_table(basis_x.T),
            left_table(basis_y),
            left_table(basis_y.T),
            right_table(basis_z.T),
            right_table(basis_z),
        )
    ]
    band_ids = jnp.arange(occupied.shape[0], dtype=jnp.int32)
    matches = band_of_slot[:, None] == band_ids[None, :]
    occupancy = jnp.sum(jnp.where(matches, occupied[None, :], 0), axis=1)
    scaled = -0.125 * occupancy.astype(jnp.float32)
    padded = jnp.pad(scaled, (0, -scaled.shape[0] % 8))
    weights = jnp.broadcast_to(padded[:, None], (padded.shape[0], LANES))
    return jnp.stack(
        [exchange(targets[t], sources, weights, tables) for t in range(targets.shape[0])]
    )


def solution(mesh):
    return jax.shard_map(
        shards,
        mesh=mesh,
        in_specs=(
            P("blk", None, None, None),
            P(("blk", "col"), None, None, None),
            P(("blk", "col")),
            P(),
        ),
        out_specs=P("blk", "col", None, None),
        check_vma=False,
    )
```

```python
import functools
import math

import jax
import jax.numpy as jnp
import ml_dtypes
import numpy as np
from jax import lax
from jax.experimental import pallas as pl
from jax.experimental.pallas import tpu as pltpu
from jax.sharding import PartitionSpec as P

HOPS = 2
LANES = 128

grid_spacing = 0.3
screening = 0.11


def frequency_sq(length):
    index_row = np.arange(length)
    periodic = np.minimum(index_row, length - index_row).astype(np.float64)
    return (2.0 * math.pi * periodic / (length * grid_spacing)) ** 2


def kernel_table(size_x, size_y, size_z):
    g_sq = (
        frequency_sq(size_x)[:, None, None]
        + frequency_sq(size_y)[None, :, None]
        + frequency_sq(size_z)[None, None, :]
    )
    safe_sq = np.where(g_sq > 0, g_sq, 1.0)
    value = 4.0 * math.pi / safe_sq * (1.0 - np.exp(-safe_sq / (4.0 * screening * screening)))
    value = np.where(g_sq > 0, value, math.pi / (screening * screening))
    padded = np.zeros((size_x, size_y, LANES), np.float32)
    padded[:, :, :size_z] = value
    return padded.reshape(size_x, size_y * LANES)


def fourier_basis(length):
    row_index = np.arange(length)[:, None]
    col_index = np.arange(length)[None, :]
    residue = row_index * col_index % length
    phase_angle = 2.0 * math.pi / length * residue
    half_length = length // 2
    basis_table = np.where(row_index <= half_length, np.cos(phase_angle), np.sin(phase_angle))
    edge_row = (row_index == 0) | (row_index == half_length)
    norm_scale = np.where(edge_row, math.sqrt(1.0 / length), math.sqrt(2.0 / length))
    return basis_table * norm_scale


def two_parts(table):
    high = table.astype(ml_dtypes.bfloat16)
    low = (table - high.astype(np.float64)).astype(ml_dtypes.bfloat16)
    return high, low


def left_table(table):
    high, low = two_parts(table)
    return np.concatenate([high, high, low], axis=1)


def right_table(table):
    high, low = two_parts(table)
    length = table.shape[0]
    out = np.zeros((2 * LANES, 2 * LANES), ml_dtypes.bfloat16)
    for start in (0, LANES):
        out[start:start + length, :length] = high
        out[start:start + length, LANES:LANES + length] = low
    return out


def split(value):
    high = value.astype(jnp.bfloat16).astype(jnp.float32)
    return high, value - high


def dot(left, right):
    return jnp.dot(left, right, preferred_element_type=jnp.float32)


def along_rows(table, value):
    high, low = split(value)
    stacked = jnp.concatenate([high, low, high], axis=0).astype(jnp.bfloat16)
    return dot(table, stacked)


def along_lanes(value, table):
    high, low = split(value)
    wide = jnp.concatenate([high, low], axis=1).astype(jnp.bfloat16)
    product = dot(wide, table)
    return product[:, :LANES] + product[:, LANES:]


def largest_divisor(length, most):
    return max(d for d in range(1, most + 1) if length % d == 0)


def exchange_kernel(
    count_blk,
    count_col,
    weight_hbm,
    target_hbm,
    source_hbm,
    *refs,
):
    tables_hbm, (out_ref,), refs = refs[:7], refs[7:8], refs[8:]
    (coulomb_ref, x_in, x_out, y_in, y_out, z_in, z_out), refs = refs[:7], refs[7:]
    (
        target_ref, held, weights, scratch, accum, landed,
        local_sem, hop_send, hop_recv, weight_send, weight_recv, part_send, part_recv,
    ) = refs
    _, count_s, size_x, size_y, size_z = held.shape
    part_x = size_x // count_col
    group_x = largest_divisor(part_x, 24)
    group_y = largest_divisor(size_y, 24)
    rows = group_x * size_y
    me_blk, me_col = lax.axis_index("blk"), lax.axis_index("col")
    right = lax.rem(me_blk + 1, count_blk)
    left = lax.rem(me_blk + count_blk - 1, count_blk)

    local = [
        pltpu.make_async_copy(source, dest, local_sem.at[index])
        for index, (source, dest) in enumerate(
            [(source_hbm, held.at[0]), (weight_hbm, weights.at[0]), (target_hbm, target_ref)]
            + list(
                zip(tables_hbm, (coulomb_ref, x_in, x_out, y_in, y_out, z_in, z_out))
            )
        )
    ]
    for copy in local:
        copy.start()

    barrier = pltpu.get_barrier_semaphore()
    others = [(right, me_col), (left, me_col)] + [
        (me_blk, lax.rem(me_col + d, count_col)) for d in range(1, count_col)
    ]
    for other in others:
        pl.semaphore_signal(
            barrier, inc=1, device_id=other, device_id_type=pl.DeviceIdType.MESH
        )
    pl.semaphore_wait(barrier, len(others))

    def hop_copies(hop):
        return [
            pltpu.make_async_remote_copy(
                src_ref=ref.at[hop],
                dst_ref=ref.at[hop + 1],
                send_sem=send.at[hop],
                recv_sem=recv.at[hop],
                device_id=(right, me_col),
                device_id_type=pl.DeviceIdType.MESH,
            )
            for ref, send, recv in (
                (held, hop_send, hop_recv), (weights, weight_send, weight_recv)
            )
        ]

    def part_copy(d):
        other = lax.rem(me_col + d, count_col)
        return pltpu.make_async_remote_copy(
            src_ref=accum.at[pl.ds(other * part_x, part_x)],
            dst_ref=landed.at[d - 1],
            send_sem=part_send.at[d - 1],
            recv_sem=part_recv.at[d - 1],
            device_id=(me_blk, other),
            device_id_type=pl.DeviceIdType.MESH,
        )

    local[0].wait()
    local[1].wait()
    for copy in hop_copies(0):
        copy.start()
    for copy in local[2:]:
        copy.wait()

    def slabs(ref, start):
        return ref[pl.ds(start, group_x)].astype(jnp.float32).reshape(rows, size_z)

    def to_spectrum(hop):
        @pl.loop(0, size_x // group_x)
        def _(step):
            start = step * group_x
            target = slabs(target_ref, start)
            for s in range(count_s):
                pair = target * slabs(held.at[hop, s], start)
                pair = jnp.concatenate(
                    [pair, jnp.zeros((rows, LANES - size_z), jnp.float32)], axis=1
                )
                pair = along_lanes(pair, z_in[...])
                wide = jnp.concatenate(
                    [pair[g * size_y:(g + 1) * size_y] for g in range(group_x)], axis=1
                )
                wide = along_rows(y_in[...], wide)
                for g in range(group_x):
                    first = pl.multiple_of((start + g) * size_y, 8)
                    scratch[s, pl.ds(first, size_y), :] = wide[:, g * LANES:(g + 1) * LANES]

        @pl.loop(0, size_y // group_y)
        def _(step):
            start = step * group_y
            columns = pl.ds(pl.multiple_of(start * LANES, LANES), group_y * LANES)
            for s in range(count_s):
                wide = jnp.concatenate(
                    [
                        scratch[s, pl.ds(start + g, size_x, stride=size_y), :]
                        for g in range(group_y)
                    ],
                    axis=1,
                )
                wide = along_rows(x_in[...], wide) * coulomb_ref[:, columns]
                wide = along_rows(x_out[...], wide)
                for g in range(group_y):
                    scratch[s, pl.ds(start + g, size_x, stride=size_y), :] = wide[
                        :, g * LANES:(g + 1) * LANES
                    ]

    def to_grid(hop, first_x, steps, fresh):
        @pl.loop(0, steps)
        def _(step):
            start = first_x + step * group_x
            total = None
            for s in range(count_s):
                wide = jnp.concatenate(
                    [
                        scratch[s, pl.ds(pl.multiple_of((start + g) * size_y, 8), size_y), :]
                        for g in range(group_x)
                    ],
                    axis=1,
                )
                wide = along_rows(y_out[...], wide)
                field = jnp.concatenate(
                    [wide[:, g * LANES:(g + 1) * LANES] for g in range(group_x)], axis=0
                )
                field = along_lanes(field, z_out[...])[:, :size_z]
                weight = weights[hop, s:s + 1, :size_z]
                term = field * (slabs(held.at[hop, s], start) * weight)
                total = term if total is None else total + term
            total = total.reshape(group_x, size_y, size_z)
            if not fresh:
                total = total + accum[pl.ds(start, group_x)]
            accum[pl.ds(start, group_x)] = total

    for hop in range(HOPS):
        to_spectrum(hop)
        to_grid(hop, 0, size_x // group_x, hop == 0)
        for copy in hop_copies(hop):
            copy.wait()
        if hop + 1 < HOPS:
            for copy in hop_copies(hop + 1):
                copy.start()

    to_spectrum(HOPS)
    for d in range(1, count_col):
        other = lax.rem(me_col + d, count_col)
        to_grid(HOPS, other * part_x, part_x // group_x, False)
        part_copy(d).start()
    to_grid(HOPS, me_col * part_x, part_x // group_x, False)
    for d in range(1, count_col):
        part_copy(d).wait()

    @pl.loop(0, part_x)
    def _(step):
        total = accum[me_col * part_x + step]
        for d in range(1, count_col):
            total = total + landed[d - 1, step]
        out_ref[step] = total


def exchange(target, sources, weights, tables):
    count_s, size_x, size_y, size_z = sources.shape
    count_blk, count_col = lax.axis_size("blk"), lax.axis_size("col")
    part_x = size_x // count_col
    operands = [weights, target, sources] + tables
    cells = size_x * size_y * size_z
    dma = pltpu.SemaphoreType.DMA
    return pl.pallas_call(
        functools.partial(exchange_kernel, count_blk, count_col),
        out_shape=jax.ShapeDtypeStruct((part_x, size_y, size_z), jnp.float32),
        in_specs=[pl.BlockSpec(memory_space=pl.ANY)] * len(operands),
        out_specs=pl.BlockSpec(memory_space=pltpu.VMEM),
        scratch_shapes=[pltpu.VMEM(table.shape, table.dtype) for table in tables]
        + [
            pltpu.VMEM(target.shape, target.dtype),
            pltpu.VMEM((HOPS + 1,) + sources.shape, sources.dtype),
            pltpu.VMEM((HOPS + 1,) + weights.shape, weights.dtype),
            pltpu.VMEM((count_s, size_x * size_y, LANES), jnp.float32),
            pltpu.VMEM((size_x, size_y, size_z), jnp.float32),
            pltpu.VMEM((max(count_col - 1, 1), part_x, size_y, size_z), jnp.float32),
            dma((len(operands),)),
            dma((HOPS,)),
            dma((HOPS,)),
            dma((HOPS,)),
            dma((HOPS,)),
            dma((max(count_col - 1, 1),)),
            dma((max(count_col - 1, 1),)),
        ],
        compiler_params=pltpu.CompilerParams(
            vmem_limit_bytes=56 * 1024 * 1024, collective_id=0, has_side_effects=True
        ),
        cost_estimate=pl.CostEstimate(
            flops=(HOPS + 1) * count_s * cells * 12 * (size_x + size_y + size_z),
            bytes_accessed=cells * (4 * count_s + 10),
            transcendentals=0,
        ),
    )(*operands)


def shards(targets, sources, band_of_slot, occupied):
    size_x, size_y, size_z = targets.shape[1:]
    basis_x, basis_y, basis_z = (fourier_basis(n) for n in (size_x, size_y, size_z))
    tables = [
        jnp.asarray(table)
        for table in (
            kernel_table(size_x, size_y, size_z),
            left_table(basis_x),
            left_table(basis_x.T),
            left_table(basis_y),
            left_table(basis_y.T),
            right_table(basis_z.T),
            right_table(basis_z),
        )
    ]
    band_ids = jnp.arange(occupied.shape[0], dtype=jnp.int32)
    matches = band_of_slot[:, None] == band_ids[None, :]
    occupancy = jnp.sum(jnp.where(matches, occupied[None, :], 0), axis=1)
    scaled = -0.125 * occupancy.astype(jnp.float32)
    padded = jnp.pad(scaled, (0, -scaled.shape[0] % 8))
    weights = jnp.broadcast_to(padded[:, None], (padded.shape[0], LANES))
    return jnp.stack(
        [exchange(targets[t], sources, weights, tables) for t in range(targets.shape[0])]
    )


def solution(mesh):
    return jax.shard_map(
        shards,
        mesh=mesh,
        in_specs=(
            P("blk", None, None, None),
            P(("blk", "col"), None, None, None),
            P(("blk", "col")),
            P(),
        ),
        out_specs=P("blk", "col", None, None),
        check_vma=False,
    )
```

```python
import functools
import math

import jax
import jax.numpy as jnp
import ml_dtypes
import numpy as np
from jax import lax
from jax.experimental import pallas as pl
from jax.experimental.pallas import tpu as pltpu
from jax.sharding import PartitionSpec as P

HOPS = 2
LANES = 128

grid_spacing = 0.3
screening = 0.11


def frequency_sq(length):
    index_row = np.arange(length)
    periodic = np.minimum(index_row, length - index_row).astype(np.float64)
    return (2.0 * math.pi * periodic / (length * grid_spacing)) ** 2


def kernel_table(size_x, size_y, size_z):
    g_sq = (
        frequency_sq(size_x)[:, None, None]
        + frequency_sq(size_y)[None, :, None]
        + frequency_sq(size_z)[None, None, :]
    )
    safe_sq = np.where(g_sq > 0, g_sq, 1.0)
    value = 4.0 * math.pi / safe_sq * (1.0 - np.exp(-safe_sq / (4.0 * screening * screening)))
    value = np.where(g_sq > 0, value, math.pi / (screening * screening))
    padded = np.zeros((size_x, size_y, LANES), np.float32)
    padded[:, :, :size_z] = value
    return padded.reshape(size_x, size_y * LANES)


def fourier_basis(length):
    row_index = np.arange(length)[:, None]
    col_index = np.arange(length)[None, :]
    residue = row_index * col_index % length
    phase_angle = 2.0 * math.pi / length * residue
    half_length = length // 2
    basis_table = np.where(row_index <= half_length, np.cos(phase_angle), np.sin(phase_angle))
    edge_row = (row_index == 0) | (row_index == half_length)
    norm_scale = np.where(edge_row, math.sqrt(1.0 / length), math.sqrt(2.0 / length))
    return basis_table * norm_scale


def two_parts(table):
    high = table.astype(ml_dtypes.bfloat16)
    low = (table - high.astype(np.float64)).astype(ml_dtypes.bfloat16)
    return high, low


def left_table(table):
    high, low = two_parts(table)
    return np.concatenate([high, high, low], axis=1)


def right_table(table):
    high, low = two_parts(table)
    length = table.shape[0]
    out = np.zeros((2 * LANES, 2 * LANES), ml_dtypes.bfloat16)
    for start in (0, LANES):
        out[start:start + length, :length] = high
        out[start:start + length, LANES:LANES + length] = low
    return out


def split(value):
    high = value.astype(jnp.bfloat16).astype(jnp.float32)
    return high, value - high


def dot(left, right):
    return jnp.dot(left, right, preferred_element_type=jnp.float32)


def along_rows(table, value):
    high, low = split(value)
    stacked = jnp.concatenate([high, low, high], axis=0).astype(jnp.bfloat16)
    return dot(table, stacked)


def along_lanes(value, table):
    high, low = split(value)
    wide = jnp.concatenate([high, low], axis=1).astype(jnp.bfloat16)
    product = dot(wide, table)
    return product[:, :LANES] + product[:, LANES:]


def largest_divisor(length, most):
    return max(d for d in range(1, most + 1) if length % d == 0)


def exchange_kernel(
    count_blk,
    count_col,
    weight_hbm,
    target_hbm,
    source_hbm,
    *refs,
):
    tables_hbm, (out_ref,), refs = refs[:7], refs[7:8], refs[8:]
    (coulomb_ref, x_in, x_out, y_in, y_out, z_in, z_out), refs = refs[:7], refs[7:]
    (
        target_ref, current, packed, weights, scratch, accum, landed,
        local_sem, hop_send, hop_recv, weight_send, weight_recv, part_send, part_recv,
    ) = refs
    count_s, size_x, size_y, size_z = current.shape
    part_x = size_x // count_col
    group_x = largest_divisor(part_x, 24)
    group_y = largest_divisor(size_y, 24)
    rows = group_x * size_y
    me_blk, me_col = lax.axis_index("blk"), lax.axis_index("col")
    right = lax.rem(me_blk + 1, count_blk)
    left = lax.rem(me_blk + count_blk - 1, count_blk)

    local = [
        pltpu.make_async_copy(source, dest, local_sem.at[index])
        for index, (source, dest) in enumerate(
            [(source_hbm, current), (weight_hbm, weights.at[0]), (target_hbm, target_ref)]
            + list(
                zip(tables_hbm, (coulomb_ref, x_in, x_out, y_in, y_out, z_in, z_out))
            )
        )
    ]
    for copy in local:
        copy.start()

    barrier = pltpu.get_barrier_semaphore()
    others = [(right, me_col), (left, me_col)] + [
        (me_blk, lax.rem(me_col + d, count_col)) for d in range(1, count_col)
    ]
    for other in others:
        pl.semaphore_signal(
            barrier, inc=1, device_id=other, device_id_type=pl.DeviceIdType.MESH
        )
    pl.semaphore_wait(barrier, len(others))

    def hop_copies(hop):
        return [
            pltpu.make_async_remote_copy(
                src_ref=ref.at[hop],
                dst_ref=ref.at[hop + 1],
                send_sem=send.at[hop],
                recv_sem=recv.at[hop],
                device_id=(right, me_col),
                device_id_type=pl.DeviceIdType.MESH,
            )
            for ref, send, recv in (
                (packed, hop_send, hop_recv), (weights, weight_send, weight_recv)
            )
        ]

    def part_copy(d):
        other = lax.rem(me_col + d, count_col)
        return pltpu.make_async_remote_copy(
            src_ref=accum.at[pl.ds(other * part_x, part_x)],
            dst_ref=landed.at[d - 1],
            send_sem=part_send.at[d - 1],
            recv_sem=part_recv.at[d - 1],
            device_id=(me_blk, other),
            device_id_type=pl.DeviceIdType.MESH,
        )

    spare = LANES - size_z
    spare_of = size_z // spare
    chunk = largest_divisor(size_x, 24)
    side = chunk // (spare_of + 1)
    main = chunk - side
    dense_rows = main * size_y

    def pack():
        @pl.loop(0, count_s)
        def _(s):
            for c in range(size_x // chunk):
                value = current[s, c * chunk:(c + 1) * chunk].astype(jnp.float32)
                extra = jnp.concatenate(
                    [value[main:, :, i * spare:(i + 1) * spare] for i in range(spare_of)], axis=0
                )
                dense = jnp.concatenate([value[:main], extra], axis=2)
                packed[0, s, c * dense_rows:(c + 1) * dense_rows] = dense.reshape(
                    dense_rows, LANES
                ).astype(packed.dtype)

    def unpack(hop):
        @pl.loop(0, count_s)
        def _(s):
            for c in range(size_x // chunk):
                dense = packed[hop, s, c * dense_rows:(c + 1) * dense_rows].astype(jnp.float32)
                dense = dense.reshape(main, size_y, LANES)
                extra = dense[:, :, size_z:]
                extra = jnp.concatenate(
                    [extra[i * side:(i + 1) * side] for i in range(spare_of)], axis=2
                )
                value = jnp.concatenate([dense[:, :, :size_z], extra], axis=0)
                current[s, c * chunk:(c + 1) * chunk] = value.astype(current.dtype)

    local[0].wait()
    local[1].wait()
    pack()
    for copy in hop_copies(0):
        copy.start()
    for copy in local[2:]:
        copy.wait()

    def slabs(ref, start):
        return ref[pl.ds(start, group_x)].astype(jnp.float32).reshape(rows, size_z)

    def to_spectrum(hop):
        @pl.loop(0, size_x // group_x)
        def _(step):
            start = step * group_x
            target = slabs(target_ref, start)
            for s in range(count_s):
                pair = target * slabs(current.at[s], start)
                pair = jnp.concatenate(
                    [pair, jnp.zeros((rows, LANES - size_z), jnp.float32)], axis=1
                )
                pair = along_lanes(pair, z_in[...])
                wide = jnp.concatenate(
                    [pair[g * size_y:(g + 1) * size_y] for g in range(group_x)], axis=1
                )
                wide = along_rows(y_in[...], wide)
                for g in range(group_x):
                    first = pl.multiple_of((start + g) * size_y, 8)
                    scratch[s, pl.ds(first, size_y), :] = wide[:, g * LANES:(g + 1) * LANES]

        @pl.loop(0, size_y // group_y)
        def _(step):
            start = step * group_y
            columns = pl.ds(pl.multiple_of(start * LANES, LANES), group_y * LANES)
            for s in range(count_s):
                wide = jnp.concatenate(
                    [
                        scratch[s, pl.ds(start + g, size_x, stride=size_y), :]
                        for g in range(group_y)
                    ],
                    axis=1,
                )
                wide = along_rows(x_in[...], wide) * coulomb_ref[:, columns]
                wide = along_rows(x_out[...], wide)
                for g in range(group_y):
                    scratch[s, pl.ds(start + g, size_x, stride=size_y), :] = wide[
                        :, g * LANES:(g + 1) * LANES
                    ]

    def to_grid(hop, first_x, steps, fresh):
        @pl.loop(0, steps)
        def _(step):
            start = first_x + step * group_x
            total = None
            for s in range(count_s):
                wide = jnp.concatenate(
                    [
                        scratch[s, pl.ds(pl.multiple_of((start + g) * size_y, 8), size_y), :]
                        for g in range(group_x)
                    ],
                    axis=1,
                )
                wide = along_rows(y_out[...], wide)
                field = jnp.concatenate(
                    [wide[:, g * LANES:(g + 1) * LANES] for g in range(group_x)], axis=0
                )
                field = along_lanes(field, z_out[...])[:, :size_z]
                weight = weights[hop, s:s + 1, :size_z]
                term = field * (slabs(current.at[s], start) * weight)
                total = term if total is None else total + term
            total = total.reshape(group_x, size_y, size_z)
            if not fresh:
                total = total + accum[pl.ds(start, group_x)]
            accum[pl.ds(start, group_x)] = total

    for hop in range(HOPS):
        to_spectrum(hop)
        to_grid(hop, 0, size_x // group_x, hop == 0)
        for copy in hop_copies(hop):
            copy.wait()
        if hop + 1 < HOPS:
            for copy in hop_copies(hop + 1):
                copy.start()
        unpack(hop + 1)

    to_spectrum(HOPS)
    for d in range(1, count_col):
        other = lax.rem(me_col + d, count_col)
        to_grid(HOPS, other * part_x, part_x // group_x, False)
        part_copy(d).start()
    to_grid(HOPS, me_col * part_x, part_x // group_x, False)
    for d in range(1, count_col):
        part_copy(d).wait()

    @pl.loop(0, part_x)
    def _(step):
        total = accum[me_col * part_x + step]
        for d in range(1, count_col):
            total = total + landed[d - 1, step]
        out_ref[step] = total


def exchange(target, sources, weights, tables):
    count_s, size_x, size_y, size_z = sources.shape
    count_blk, count_col = lax.axis_size("blk"), lax.axis_size("col")
    part_x = size_x // count_col
    operands = [weights, target, sources] + tables
    cells = size_x * size_y * size_z
    dma = pltpu.SemaphoreType.DMA
    return pl.pallas_call(
        functools.partial(exchange_kernel, count_blk, count_col),
        out_shape=jax.ShapeDtypeStruct((part_x, size_y, size_z), jnp.float32),
        in_specs=[pl.BlockSpec(memory_space=pl.ANY)] * len(operands),
        out_specs=pl.BlockSpec(memory_space=pltpu.VMEM),
        scratch_shapes=[pltpu.VMEM(table.shape, table.dtype) for table in tables]
        + [
            pltpu.VMEM(target.shape, target.dtype),
            pltpu.VMEM(sources.shape, sources.dtype),
            pltpu.VMEM((HOPS + 1, count_s, cells // LANES, LANES), sources.dtype),
            pltpu.VMEM((HOPS + 1,) + weights.shape, weights.dtype),
            pltpu.VMEM((count_s, size_x * size_y, LANES), jnp.float32),
            pltpu.VMEM((size_x, size_y, size_z), jnp.float32),
            pltpu.VMEM((max(count_col - 1, 1), part_x, size_y, size_z), jnp.float32),
            dma((len(operands),)),
            dma((HOPS,)),
            dma((HOPS,)),
            dma((HOPS,)),
            dma((HOPS,)),
            dma((max(count_col - 1, 1),)),
            dma((max(count_col - 1, 1),)),
        ],
        compiler_params=pltpu.CompilerParams(
            vmem_limit_bytes=56 * 1024 * 1024, collective_id=0, has_side_effects=True
        ),
        cost_estimate=pl.CostEstimate(
            flops=(HOPS + 1) * count_s * cells * 12 * (size_x + size_y + size_z),
            bytes_accessed=cells * (4 * count_s + 10),
            transcendentals=0,
        ),
    )(*operands)


def shards(targets, sources, band_of_slot, occupied):
    size_x, size_y, size_z = targets.shape[1:]
    basis_x, basis_y, basis_z = (fourier_basis(n) for n in (size_x, size_y, size_z))
    tables = [
        jnp.asarray(table)
        for table in (
            kernel_table(size_x, size_y, size_z),
            left_table(basis_x),
            left_table(basis_x.T),
            left_table(basis_y),
            left_table(basis_y.T),
            right_table(basis_z.T),
            right_table(basis_z),
        )
    ]
    band_ids = jnp.arange(occupied.shape[0], dtype=jnp.int32)
    matches = band_of_slot[:, None] == band_ids[None, :]
    occupancy = jnp.sum(jnp.where(matches, occupied[None, :], 0), axis=1)
    scaled = -0.125 * occupancy.astype(jnp.float32)
    padded = jnp.pad(scaled, (0, -scaled.shape[0] % 8))
    weights = jnp.broadcast_to(padded[:, None], (padded.shape[0], LANES))
    return jnp.stack(
        [exchange(targets[t], sources, weights, tables) for t in range(targets.shape[0])]
    )


def solution(mesh):
    return jax.shard_map(
        shards,
        mesh=mesh,
        in_specs=(
            P("blk", None, None, None),
            P(("blk", "col"), None, None, None),
            P(("blk", "col")),
            P(),
        ),
        out_specs=P("blk", "col", None, None),
        check_vma=False,
    )
```
